256 devices in a mesh: row: 8 (over y, x_hi), col: 32 (over x_lo, z, core).
Axes of the slice: x: 4 (x_hi: 2, x_lo: 2; x = x_hi * 2 + x_lo), y: 4, z: 8, core: 2. Of those that a mesh axis runs over, the one named last changes fastest.
Arguments:
- pair: bfloat16 [2560, 2560, 128], P('row', 'col'), may hold values from -6 to 6
- in_gain: float32 [128], replicated, may hold values from 0.1 to 1.9
- a_weight: bfloat16 [128, 256], replicated, may hold values from -0.5 to 0.5
- b_weight: bfloat16 [128, 256], replicated, may hold values from -0.5 to 0.5
- gate_weight: bfloat16 [128, 128], replicated, may hold values from -0.5 to 0.5
- out_gain: float32 [128], replicated, may hold values from 0.1 to 1.9
- out_weight: bfloat16 [128, 128], replicated, may hold values from -0.5 to 0.5
Outputs:
- mixed: bfloat16 [256, 2560, 128], P('row', 'col')
The draws below stay inside these ranges and needn't reach their ends.
All inputs are finite; a program needn't handle non-finite values.
Results may differ from the reference program's by a relative error of at most 0.0078.
Values may be sent and summed in bfloat16 or wider, within the bound.
A program may use at most 192 MiB of HBM per device.

```python
import jax
import jax.numpy as jnp
from jax import lax

C = 128
CH = 128
COLS_DEV = 80
WIN_BLOCK = 8
TOKENS = 2560
WINDOW = 256
N_COL = 32


def block_scale(own_key, extent, cuts, smallest, largest):
    def one(position, parts):
        draws = jax.random.uniform(jax.random.fold_in(jax.random.fold_in(own_key, 6), position), (parts,), jnp.float32, smallest / len(cuts), largest / len(cuts))
        return jnp.repeat(jnp.exp(draws), extent[position] // parts).reshape((-1,) + (1,) * (len(extent) - position - 1))

    level = one(*cuts[0])
    for cut in cuts[1:]:
        level = level * one(*cut)
    return level


def normal_values(own_key, dims, width, reach, pieces=(), held_as=jnp.bfloat16):
    level = block_scale(own_key, dims, pieces, -0.22, 0.18) if pieces else 1.0
    result = jax.random.normal(own_key, dims, jnp.float32) * width * level
    return jnp.minimum(jnp.maximum(result, -reach), reach).astype(held_as)


def setup_inputs(seed: int = 0) -> dict:
    key_of = jax.random.split(jax.random.key(seed), 8)
    pair = normal_values(key_of[0], (TOKENS, TOKENS, C), 1.0, 6.0, ((0, 8), (1, 32)))
    in_gain = jnp.clip(1.0 + 0.18 * jax.random.normal(key_of[1], (C,), jnp.float32), 0.1, 1.9)
    a_weight = normal_values(key_of[2], (C, 2 * CH), C ** -0.5, 0.5)
    b_weight = normal_values(key_of[3], (C, 2 * CH), C ** -0.5, 0.5)
    gate_weight = normal_values(key_of[4], (C, C), C ** -0.5, 0.5)
    out_gain = jnp.clip(1.0 + 0.18 * jax.random.normal(key_of[5], (CH,), jnp.float32), 0.1, 1.9)
    out_weight = normal_values(key_of[6], (CH, C), CH ** -0.5, 0.5)
    return {"pair": pair, "in_gain": in_gain, "a_weight": a_weight, "b_weight": b_weight, "gate_weight": gate_weight, "out_gain": out_gain, "out_weight": out_weight}


def layer_norm(values, scales):
    floats = values.astype(jnp.float32)
    center = floats - lax.optimization_barrier(jnp.mean(floats, axis=-1, keepdims=True))
    spread = lax.optimization_barrier(jnp.mean(center * center, axis=-1, keepdims=True))
    return center * lax.rsqrt(spread + 1e-05) * scales

def gated_proj(inputs, weight):
    joined = jnp.einsum('rjc,ch->rjh', inputs.astype(jnp.float32), weight.astype(jnp.float32))
    split_at = weight.shape[1] // 2
    return (jax.nn.sigmoid(joined[..., split_at:]) * joined[..., :split_at]).astype(jnp.bfloat16)

def window_cols(array):
    lead = array.shape[0]
    shaped = array.reshape(lead, N_COL, COLS_DEV, array.shape[-1])
    return shaped[:, :, :WIN_BLOCK].reshape(lead, WINDOW, array.shape[-1])

def reference(pair, in_gain, a_weight, b_weight, gate_weight, out_gain, out_weight):
    blocked = pair.reshape(TOKENS // COLS_DEV, COLS_DEV, TOKENS, C)

    def accumulate(total, slab):
        normed = layer_norm(slab, in_gain).astype(jnp.bfloat16)
        left_proj = gated_proj(window_cols(normed), a_weight)
        right_proj = gated_proj(normed, b_weight)
        added = jnp.einsum('kwh,kjh->wjh', left_proj.astype(jnp.float32), right_proj.astype(jnp.float32))
        return (total + added, None)
    start_sum = jnp.zeros((WINDOW, TOKENS, CH), jnp.float32)
    summed, unused = lax.scan(accumulate, start_sum, blocked)
    win_pair = pair.reshape(N_COL, COLS_DEV, TOKENS, C)[:, :WIN_BLOCK].reshape(WINDOW, TOKENS, C)
    win_normed = layer_norm(win_pair, in_gain).astype(jnp.bfloat16)
    gate_vals = jax.nn.sigmoid(jnp.einsum('wjc,cd->wjd', win_normed.astype(jnp.float32), gate_weight.astype(jnp.float32)))
    update_in = layer_norm(summed, out_gain).astype(jnp.bfloat16)
    projected = jnp.einsum('wjh,hc->wjc', update_in.astype(jnp.float32), out_weight.astype(jnp.float32))
    return (gate_vals * projected).astype(jnp.bfloat16)
```

```python
import functools

import jax
import jax.numpy as jnp
from jax import lax
from jax.experimental import pallas as pl
from jax.experimental.pallas import tpu as pltpu
from jax.sharding import PartitionSpec as P

MESH = pl.DeviceIdType.MESH
BF = jnp.bfloat16
F32 = jnp.float32
EPS = 1e-05
KB = 16


def sigmoid(v):
    return 0.5 * jnp.tanh(0.5 * v) + 0.5


def norm_lanes(v, gain):
    f = v.astype(F32)
    f = f - jnp.mean(f, axis=-1, keepdims=True)
    spread = jnp.mean(f * f, axis=-1, keepdims=True)
    return f * lax.rsqrt(spread + EPS) * gain


def dot_nt(a, b):
    return lax.dot_general(a, b, (((1,), (1,)), ((), ())), preferred_element_type=F32)


def kernel(pair, in_gain, a_w, b_w, g_w, out_gain, o_w, out,
           win, pbuf, gwin, wat, wbt, t1, t2, tr, lbuf, rbuf, sbuf, ybuf, xhs, xhr, fbuf, ubuf, gates,
           win_sem, p_sem, g_sem, zs, zr, xs_, xr, cs, cr, ys, yr, hs, hr):
    row = lax.axis_index("row")
    col = lax.axis_index("col")
    y, xh = row // 2, row % 2
    x, z, c = col // 16, (col // 2) % 8, col % 2

    def dev(y_, xh_, x_, z_, c_):
        return (y_ * 2 + xh_, (x_ * 8 + z_) * 2 + c_)

    up = dev(y, xh, x, (z + 1) % 8, c)
    down = dev(y, xh, x, (z + 7) % 8, c)
    across = dev(y, xh, 1 - x, z, c)
    mate = dev(y, xh, x, z, 1 - c)
    twin = dev(y, 1 - xh, x, z, c)
    others = [dev((y + d) % 4, xh, x, z, c) for d in (1, 2, 3)]

    win_copy = pltpu.make_async_copy(pair.at[:, 0:16, :], win, win_sem)
    win_copy.start()

    def p_copy(step):
        slot = step % 2
        return pltpu.make_async_copy(pair.at[pl.ds(step * KB, KB)], pbuf.at[slot], p_sem.at[slot])

    p_copy(0).start()
    g_copies = [pltpu.make_async_copy(pair.at[80 * b:80 * b + 8], gwin.at[b], g_sem.at[b]) for b in range(4)]
    for copy in g_copies:
        copy.start()

    barrier = pltpu.get_barrier_semaphore()
    for d in [up, down, across, mate, twin] + others:
        pl.semaphore_signal(barrier, inc=1, device_id=d, device_id_type=MESH)

    lane = lax.broadcasted_iota(jnp.int32, (8, 128), 1)
    lane16 = lax.broadcasted_iota(jnp.int32, (16, 128), 1)
    gain = in_gain[...]

    wat[...] = a_w[...].astype(F32).T.astype(BF)
    t2[0:256, :] = b_w[...].astype(F32).T
    wbt[0:128, :] = t2[pl.ds(0, 128, stride=2), :].astype(BF)
    wbt[128:256, :] = t2[pl.ds(1, 128, stride=2), :].astype(BF)

    win_copy.wait()

    @pl.loop(0, 10)
    def _(i):
        v = win[pl.ds(i * 32, 32)].astype(F32)[:, 0:8, :]
        t1[pl.ds(pl.multiple_of(i * 256, 256), 256), :] = norm_lanes(v, gain).reshape(256, 128)

    t1[2560:3072, :] = jnp.zeros((512, 128), F32)
    for w in range(8):
        xw = t1[pl.ds(w, 384, stride=8), :].astype(BF)
        v = dot_nt(wat[...], xw)
        v = sigmoid(v[128:]) * v[:128]
        for t in range(3):
            t2[pl.ds(1024 * t + w, 128, stride=8), :] = v[:, t * 128:(t + 1) * 128]

    def slot(x_, z_, c_):
        return (x_ * 8 + z_) * 2 + c_

    mine = slot(x, z, c)

    @pl.loop(0, 32)
    def _(q):
        base = pl.multiple_of(q * 32, 32)
        lbuf[mine, q, 0:32, :] = t2[pl.ds(base, 32), :].astype(BF)
        lbuf[mine, q, 32:64, :] = t2[pl.ds(1024 + base, 32), :].astype(BF)
        low = t2[pl.ds(2048 + base, 16), :]
        high = pltpu.roll(t2[pl.ds(2048 + base + 16, 16), :], 64, 1)
        lbuf[mine, q, 64:80, :] = jnp.where(lane16 < 64, low, high).astype(BF)

    pl.semaphore_wait(barrier, 8)

    A, B = (0, 16), (16, 16)
    CU, CD = (0, 8), (8, 8)

    def part(x_, z_, c_, piece):
        return lbuf.at[slot(x_, z_, c_), pl.ds(piece[0], piece[1])]

    def z_copy(direction, n, k):
        origin = (z + 8 - n) % 8 if direction == 0 else (z + n) % 8
        if k == 2:
            piece = A if n < 3 else (CU if direction == 0 else CD)
            ref = part(1 - x, origin, c, piece)
        else:
            ref = part(x, origin, c, (A, B)[k])
        return pltpu.make_async_remote_copy(
            src_ref=ref, dst_ref=ref, send_sem=zs.at[direction, n, k], recv_sem=zr.at[direction, n, k],
            device_id=up if direction == 0 else down, device_id_type=MESH)

    def z_arrival(direction, n, k):
        origin = (z + 8 - (n + 1)) % 8 if direction == 0 else (z + n + 1) % 8
        if k == 2:
            piece = A if n < 3 else (CU if direction == 0 else CD)
            ref = part(1 - x, origin, c, piece)
        else:
            ref = part(x, origin, c, (A, B)[k])
        return pltpu.make_async_remote_copy(
            src_ref=ref, dst_ref=ref, send_sem=zs.at[direction, n, k], recv_sem=zr.at[direction, n, k],
            device_id=up if direction == 0 else down, device_id_type=MESH)

    def at(o):
        return (z + o) % 8

    def x_copy(o, piece, k):
        ref = part(x, at(o), c, piece)
        return pltpu.make_async_remote_copy(
            src_ref=ref, dst_ref=ref, send_sem=xs_.at[k], recv_sem=xr.at[k], device_id=across, device_id_type=MESH)

    def x_arrival(o, piece, k):
        ref = part(1 - x, at(o), c, piece)
        return pltpu.make_async_remote_copy(
            src_ref=ref, dst_ref=ref, send_sem=xs_.at[k], recv_sem=xr.at[k], device_id=across, device_id_type=MESH)

    def c_copy(side, o, piece, k):
        ref = part(x if side == 0 else 1 - x, at(o), c, piece)
        return pltpu.make_async_remote_copy(
            src_ref=ref, dst_ref=ref, send_sem=cs.at[side, o, k], recv_sem=cr.at[side, o, k],
            device_id=mate, device_id_type=MESH)

    def c_arrival(side, o, piece, k):
        ref = part(x if side == 0 else 1 - x, at(o), 1 - c, piece)
        return pltpu.make_async_remote_copy(
            src_ref=ref, dst_ref=ref, send_sem=cs.at[side, o, k], recv_sem=cr.at[side, o, k],
            device_id=mate, device_id_type=MESH)

    sent = []

    def go(copy):
        copy.start()
        sent.append(copy)

    def c_pieces(side, o):
        if side == 1 and o == 4:
            return [(CU, 0), (CD, 2), (B, 1)]
        return [(A, 0), (B, 1)]

    def serve(n, k):
        for direction in (0, 1):
            if n == 3 and k == (1 if direction == 0 else 0):
                continue
            z_arrival(direction, n, k).wait_recv()
            if n < 2 or (n == 2 and not k == (1 if direction == 0 else 0)):
                go(z_copy(direction, n + 1, k))
            o = (8 - (n + 1)) % 8 if direction == 0 else n + 1
            if k == 0:
                go(c_copy(0, o, A, 0))
            elif k == 1:
                go(x_copy(o, B, o))
                go(c_copy(0, o, B, 1))
            elif n < 3:
                go(c_copy(1, o, A, 0))
            else:
                go(c_copy(1, o, CU if direction == 0 else CD, 0 if direction == 0 else 2))

    def serve_x(o):
        x_arrival(o, B, o).wait_recv()
        go(c_copy(1, o, B, 1))

    def have(o):
        for side in (0, 1):
            for piece, k in c_pieces(side, o):
                c_arrival(side, o, piece, k).wait_recv()

    go(x_copy(0, A, 8))
    for direction in (0, 1):
        go(z_copy(direction, 0, 0))
    for direction in (0, 1):
        go(z_copy(direction, 0, 1))
    go(x_copy(0, B, 0))
    go(c_copy(0, 0, A, 0))
    go(c_copy(0, 0, B, 1))

    rbuf[:, 0, 320:384, :] = jnp.zeros((32, 64, 256), BF)
    rbuf[:, 1, 256:320, :] = jnp.zeros((32, 64, 256), BF)

    def right_step(step, tail):
        @pl.when(step + 1 < 20)
        def _():
            p_copy(step + 1).start()

        p_copy(step).wait()
        here = step % 2
        for pairs in range(KB // 2):
            first, second = [], []
            for kk in (2 * pairs, 2 * pairs + 1):
                v = norm_lanes(pbuf[here, kk], gain).astype(BF)
                main, rest = v[0:64], v[64:80]
                first += [main, rest, rest, rest, rest]
                second += [rest, rest, rest, rest, main]
            for par, rows in ((0, first), (1, second)):
                v = dot_nt(wbt[par * 128:(par + 1) * 128, :], jnp.concatenate(rows, axis=0))
                v = sigmoid(v[64:]) * v[:64]
                for half in (0, 1):
                    tr[pl.ds(par * 1024 + 2 * pairs + half, 64, stride=KB), :] = v[:, half * 128:(half + 1) * 128]
        for par in (0, 1):
            v = tr[par * 1024:(par + 1) * 1024, :].astype(BF).reshape(32, 2, KB, 128)
            base = pl.multiple_of(step * KB, KB)
            for i in (0, 1):
                where = base + 64 if (tail and i == 1) else base
                rbuf[:, i, pl.ds(pl.multiple_of(where, KB), KB), par * 128:(par + 1) * 128] = v[:, i]

    def right_steps(lo, hi, tail=False):
        @pl.loop(lo, hi)
        def _(step):
            right_step(step, tail)

    right_steps(0, 5)
    x_arrival(0, A, 8).wait_recv()
    for direction in (0, 1):
        go(z_copy(direction, 0, 2))
    go(c_copy(1, 0, A, 0))
    right_steps(5, 9)
    serve(0, 0)
    right_steps(9, 13)
    serve_x(0)
    serve(0, 1)
    right_steps(13, 16)
    right_steps(16, 20, True)
    serve(0, 2)
    serve_x(1)
    serve_x(7)

    for copy in g_copies:
        copy.wait()

    @pl.loop(0, 32)
    def _(i):
        v = norm_lanes(gwin[i // 8, i % 8], gain).astype(BF)
        gates[i] = sigmoid(jnp.dot(v, g_w[...], preferred_element_type=F32))

    def contract(chips):
        @pl.loop(0, 16)
        def _(o):
            tails = [[None, None] for _ in chips]
            for m in range(4):
                q, i = o * 2 + m // 2, m % 2
                lhs = []
                for lane_tile in range(3):
                    start = 64 if lane_tile == 2 else 32 * lane_tile + 16 * i
                    lhs.append(jnp.concatenate(
                        [lbuf[slot(cx, cz, cc), q, start:start + 16, :] for cx, cz in chips for cc in (0, 1)], axis=0))
                res = jnp.dot(jnp.concatenate(lhs, axis=1), rbuf[q, i], preferred_element_type=F32)
                for ci, (cx, cz) in enumerate(chips):
                    both = []
                    for cc in (0, 1):
                        base = (ci * 2 + cc) * 16
                        even = res[base:base + 8, 0:128]
                        odd = res[base + 8:base + 16, 128:256]
                        both.append(jnp.where(lane < 64, even, odd))
                        mix = jnp.where(lane < 64, odd, even)
                        old = tails[ci][cc]
                        tails[ci][cc] = mix if old is None else jnp.where((lane % 64) // 16 == m, mix, old)
                    sbuf[cx * 8 + cz, o, 16 * m:16 * m + 16, :] = jnp.concatenate(both, axis=0).astype(BF)
            for ci, (cx, cz) in enumerate(chips):
                sbuf[cx * 8 + cz, o, 64:80, :] = jnp.concatenate(tails[ci], axis=0).astype(BF)

    def y_copy(cx, cz):
        target = cx * 2 + cz // 4
        rel = (y + 4 - target) % 4
        return target, pltpu.make_async_remote_copy(
            src_ref=sbuf.at[cx * 8 + cz], dst_ref=ybuf.at[rel, cz % 4],
            send_sem=ys.at[cx * 8 + cz], recv_sem=yr.at[rel, cz % 4],
            device_id=dev(target, xh, x, z, c), device_id_type=MESH)

    def send_sums(cx, cz):
        target, copy = y_copy(cx, cz)

        @pl.when(target != y)
        def _():
            copy.start()

    def group(offsets):
        chips = [(cx, at(o)) for o in offsets for cx in (0, 1)]
        contract(chips)
        for cx, cz in chips:
            send_sums(cx, cz)

    have(0)
    group([0])
    serve(1, 0)
    serve(1, 1)
    have(1)
    have(7)
    group([1, 7])
    serve(1, 2)
    serve_x(2)
    serve_x(6)
    serve(2, 0)
    have(2)
    have(6)
    group([2, 6])
    serve(2, 1)
    serve(2, 2)
    serve_x(3)
    serve_x(5)
    have(3)
    have(5)
    group([3, 5])
    serve(3, 0)
    serve(3, 1)
    serve(3, 2)
    serve_x(4)
    have(4)
    group([4])

    def total(zi, o):
        v = sbuf[(y // 2) * 8 + (y % 2) * 4 + zi, o].astype(F32)
        for rel in (1, 2, 3):
            v += ybuf[rel, zi, o].astype(F32)
        return v

    def y_wait(zi):
        for rel in (1, 2, 3):
            pltpu.make_async_remote_copy(
                src_ref=ybuf.at[rel, zi], dst_ref=ybuf.at[rel, zi], send_sem=ys.at[0], recv_sem=yr.at[rel, zi],
                device_id=twin, device_id_type=MESH).wait_recv()

    def h_copy(zz):
        return pltpu.make_async_remote_copy(
            src_ref=xhs.at[zz], dst_ref=xhr.at[zz], send_sem=hs.at[zz], recv_sem=hr.at[zz],
            device_id=twin, device_id_type=MESH)

    for zz in (0, 1):
        zi = (1 - xh) * 2 + zz
        y_wait(zi)

        @pl.loop(0, 16)
        def _(o):
            xhs[zz, o] = total(zi, o).astype(BF)

        go(h_copy(zz))

    for zz in (0, 1):
        zi = xh * 2 + zz
        y_wait(zi)

        @pl.loop(0, 16)
        def _(o):
            fbuf[zz, o] = total(zi, o)

    gain_col = jnp.broadcast_to(out_gain[...], (128, 128)).T

    for zz in (0, 1):
        h_copy(zz).wait_recv()

        @pl.loop(0, 16)
        def _(o):
            v = fbuf[zz, o] + xhr[zz, o].astype(F32)
            rest = v[64:80]
            for m in range(4):
                main = v[16 * m:16 * m + 16]
                even = jnp.where(lane16 < 64, main, pltpu.roll(rest, (128 - 16 * m) % 128, 1))
                odd = jnp.where(lane16 < 64, pltpu.roll(main, 64, 1), pltpu.roll(rest, 64 - 16 * m, 1))
                base = (o * 8 + 2 * m) * 16
                ubuf[pl.ds(pl.multiple_of(base, 16), 16), :] = even
                ubuf[pl.ds(pl.multiple_of(base + 16, 16), 16), :] = odd

        @pl.loop(0, 16)
        def _(r):
            u = ubuf[pl.ds(r, 128, stride=16), :]
            u = u - jnp.mean(u, axis=0, keepdims=True)
            spread = jnp.mean(u * u, axis=0, keepdims=True)
            u = (u * lax.rsqrt(spread + EPS) * gain_col).T[0:80].astype(BF)
            v = jnp.dot(u, o_w[...], preferred_element_type=F32)
            out[zz * 16 + r] = (gates[zz * 16 + r] * v).astype(BF)

    for copy in sent:
        copy.wait_send()
    for cx in (0, 1):
        for o in range(8):
            target, copy = y_copy(cx, at(o))

            @pl.when(target != y)
            def _():
                copy.wait_send()


def step(pair, in_gain, a_w, b_w, g_w, out_gain, o_w):
    vmem = pl.BlockSpec(memory_space=pltpu.VMEM)
    dma = pltpu.SemaphoreType.DMA
    return pl.pallas_call(
        kernel,
        out_shape=jax.ShapeDtypeStruct((32, 80, 128), BF),
        in_specs=[pl.BlockSpec(memory_space=pl.ANY)] + [vmem] * 6,
        out_specs=vmem,
        scratch_shapes=[
            pltpu.VMEM((320, 16, 128), BF),
            pltpu.VMEM((2, KB, 80, 128), BF),
            pltpu.VMEM((4, 8, 80, 128), BF),
            pltpu.VMEM((256, 128), BF),
            pltpu.VMEM((256, 128), BF),
            pltpu.VMEM((3072, 128), F32),
            pltpu.VMEM((3072, 128), F32),
            pltpu.VMEM((2048, 128), F32),
            pltpu.VMEM((32, 32, 80, 128), BF),
            pltpu.VMEM((32, 2, 384, 256), BF),
            pltpu.VMEM((16, 16, 80, 128), BF),
            pltpu.VMEM((4, 4, 16, 80, 128), BF),
            pltpu.VMEM((2, 16, 80, 128), BF),
            pltpu.VMEM((2, 16, 80, 128), BF),
            pltpu.VMEM((2, 16, 80, 128), F32),
            pltpu.VMEM((2048, 128), F32),
            pltpu.VMEM((32, 80, 128), F32),
            dma, dma((2,)), dma((4,)),
            dma((2, 4, 3)), dma((2, 4, 3)),
            dma((9,)), dma((9,)),
            dma((2, 8, 3)), dma((2, 8, 3)),
            dma((16,)), dma((4, 4)),
            dma((2,)), dma((2,)),
        ],
        compiler_params=pltpu.CompilerParams(
            collective_id=0, has_side_effects=True, vmem_limit_bytes=63 * 2 ** 20),
        name="triangle",
    )(pair, in_gain.reshape(1, 128), a_w, b_w, g_w, out_gain.reshape(1, 128), o_w)


def solution(mesh):
    in_specs = (P("row", "col", None), P(), P(), P(), P(), P(), P())
    return jax.shard_map(step, mesh=mesh, in_specs=in_specs, out_specs=P("row", "col", None), check_vma=False)
```

```python
import functools

import jax
import jax.numpy as jnp
from jax import lax
from jax.experimental import pallas as pl
from jax.experimental.pallas import tpu as pltpu
from jax.sharding import PartitionSpec as P

MESH = pl.DeviceIdType.MESH
BF = jnp.bfloat16
F32 = jnp.float32
EPS = 1e-05
KB = 16


def sigmoid(v):
    return 0.5 * jnp.tanh(0.5 * v) + 0.5


def norm_lanes(v, gain):
    f = v.astype(F32)
    f = f - jnp.mean(f, axis=-1, keepdims=True)
    spread = jnp.mean(f * f, axis=-1, keepdims=True)
    return f * lax.rsqrt(spread + EPS) * gain


def dot_nt(a, b):
    return lax.dot_general(a, b, (((1,), (1,)), ((), ())), preferred_element_type=F32)


def kernel(pair, in_gain, a_w, b_w, g_w, out_gain, o_w, out,
           win, pbuf, gwin, wat, wbt, t1, t2, tr, lbuf, rbuf, sbuf, ybuf, xhs, xhr, fbuf, ubuf, gates,
           win_sem, p_sem, g_sem, zs, zr, xs_, xr, cs, cr, ys, yr, hs, hr):
    row = lax.axis_index("row")
    col = lax.axis_index("col")
    y, xh = row // 2, row % 2
    x, z, c = col // 16, (col // 2) % 8, col % 2

    def dev(y_, xh_, x_, z_, c_):
        return (y_ * 2 + xh_, (x_ * 8 + z_) * 2 + c_)

    up = dev(y, xh, x, (z + 1) % 8, c)
    down = dev(y, xh, x, (z + 7) % 8, c)
    across = dev(y, xh, 1 - x, z, c)
    mate = dev(y, xh, x, z, 1 - c)
    twin = dev(y, 1 - xh, x, z, c)
    others = [dev((y + d) % 4, xh, x, z, c) for d in (1, 2, 3)]

    win_copy = pltpu.make_async_copy(pair.at[:, 0:16, :], win, win_sem)
    win_copy.start()

    def p_copy(step):
        slot = step % 2
        return pltpu.make_async_copy(pair.at[pl.ds(step * KB, KB)], pbuf.at[slot], p_sem.at[slot])

    p_copy(0).start()
    g_copies = [pltpu.make_async_copy(pair.at[80 * b:80 * b + 8], gwin.at[b], g_sem.at[b]) for b in range(4)]
    for copy in g_copies:
        copy.start()

    barrier = pltpu.get_barrier_semaphore()
    for d in [up, down, across, mate, twin] + others:
        pl.semaphore_signal(barrier, inc=1, device_id=d, device_id_type=MESH)

    lane = lax.broadcasted_iota(jnp.int32, (8, 128), 1)
    lane16 = lax.broadcasted_iota(jnp.int32, (16, 128), 1)
    gain = in_gain[...]

    wat[...] = a_w[...].astype(F32).T.astype(BF)
    t2[0:256, :] = b_w[...].astype(F32).T
    wbt[0:128, :] = t2[pl.ds(0, 128, stride=2), :].astype(BF)
    wbt[128:256, :] = t2[pl.ds(1, 128, stride=2), :].astype(BF)

    win_copy.wait()

    @pl.loop(0, 10)
    def _(i):
        v = win[pl.ds(i * 32, 32)].astype(F32)[:, 0:8, :]
        t1[pl.ds(pl.multiple_of(i * 256, 256), 256), :] = norm_lanes(v, gain).reshape(256, 128)

    t1[2560:3072, :] = jnp.zeros((512, 128), F32)
    for w in range(8):
        xw = t1[pl.ds(w, 384, stride=8), :].astype(BF)
        v = dot_nt(wat[...], xw)
        v = sigmoid(v[128:]) * v[:128]
        for t in range(3):
            t2[pl.ds(1024 * t + w, 128, stride=8), :] = v[:, t * 128:(t + 1) * 128]

    def slot(x_, z_, c_):
        return (x_ * 8 + z_) * 2 + c_

    mine = slot(x, z, c)

    @pl.loop(0, 32)
    def _(q):
        base = pl.multiple_of(q * 32, 32)
        lbuf[mine, q, 0:32, :] = t2[pl.ds(base, 32), :].astype(BF)
        lbuf[mine, q, 32:64, :] = t2[pl.ds(1024 + base, 32), :].astype(BF)
        low = t2[pl.ds(2048 + base, 16), :]
        high = pltpu.roll(t2[pl.ds(2048 + base + 16, 16), :], 64, 1)
        lbuf[mine, q, 64:80, :] = jnp.where(lane16 < 64, low, high).astype(BF)

    pl.semaphore_wait(barrier, 8)

    A, B = (0, 16), (16, 16)
    CU, CD = (0, 8), (8, 8)

    def part(x_, z_, c_, piece):
        return lbuf.at[slot(x_, z_, c_), pl.ds(piece[0], piece[1])]

    def z_copy(direction, n, k):
        origin = (z + 8 - n) % 8 if direction == 0 else (z + n) % 8
        if k == 2:
            piece = A if n < 3 else (CU if direction == 0 else CD)
            ref = part(1 - x, origin, c, piece)
        else:
            ref = part(x, origin, c, (A, B)[k])
        return pltpu.make_async_remote_copy(
            src_ref=ref, dst_ref=ref, send_sem=zs.at[direction, n, k], recv_sem=zr.at[direction, n, k],
            device_id=up if direction == 0 else down, device_id_type=MESH)

    def z_arrival(direction, n, k):
        origin = (z + 8 - (n + 1)) % 8 if direction == 0 else (z + n + 1) % 8
        if k == 2:
            piece = A if n < 3 else (CU if direction == 0 else CD)
            ref = part(1 - x, origin, c, piece)
        else:
            ref = part(x, origin, c, (A, B)[k])
        return pltpu.make_async_remote_copy(
            src_ref=ref, dst_ref=ref, send_sem=zs.at[direction, n, k], recv_sem=zr.at[direction, n, k],
            device_id=up if direction == 0 else down, device_id_type=MESH)

    def at(o):
        return (z + o) % 8

    def x_copy(o, piece, k):
        ref = part(x, at(o), c, piece)
        return pltpu.make_async_remote_copy(
            src_ref=ref, dst_ref=ref, send_sem=xs_.at[k], recv_sem=xr.at[k], device_id=across, device_id_type=MESH)

    def x_arrival(o, piece, k):
        ref = part(1 - x, at(o), c, piece)
        return pltpu.make_async_remote_copy(
            src_ref=ref, dst_ref=ref, send_sem=xs_.at[k], recv_sem=xr.at[k], device_id=across, device_id_type=MESH)

    def c_copy(side, o, piece, k):
        ref = part(x if side == 0 else 1 - x, at(o), c, piece)
        return pltpu.make_async_remote_copy(
            src_ref=ref, dst_ref=ref, send_sem=cs.at[side, o, k], recv_sem=cr.at[side, o, k],
            device_id=mate, device_id_type=MESH)

    def c_arrival(side, o, piece, k):
        ref = part(x if side == 0 else 1 - x, at(o), 1 - c, piece)
        return pltpu.make_async_remote_copy(
            src_ref=ref, dst_ref=ref, send_sem=cs.at[side, o, k], recv_sem=cr.at[side, o, k],
            device_id=mate, device_id_type=MESH)

    sent = []

    def go(copy):
        copy.start()
        sent.append(copy)

    def c_pieces(side, o):
        if side == 1 and o == 4:
            return [(CU, 0), (CD, 2), (B, 1)]
        return [(A, 0), (B, 1)]

    def serve(n, k):
        for direction in (0, 1):
            if n == 3 and k == (1 if direction == 0 else 0):
                continue
            z_arrival(direction, n, k).wait_recv()
            if n < 2 or (n == 2 and not k == (1 if direction == 0 else 0)):
                go(z_copy(direction, n + 1, k))
            o = (8 - (n + 1)) % 8 if direction == 0 else n + 1
            if k == 0:
                go(c_copy(0, o, A, 0))
            elif k == 1:
                go(x_copy(o, B, o))
                go(c_copy(0, o, B, 1))
            elif n < 3:
                go(c_copy(1, o, A, 0))
            else:
                go(c_copy(1, o, CU if direction == 0 else CD, 0 if direction == 0 else 2))

    def serve_x(o):
        x_arrival(o, B, o).wait_recv()
        go(c_copy(1, o, B, 1))

    def have(o, half):
        for side in (0, 1):
            for piece, k in c_pieces(side, o):
                if (k == 1) == (half == 1):
                    c_arrival(side, o, piece, k).wait_recv()

    go(x_copy(0, A, 8))
    for direction in (0, 1):
        go(z_copy(direction, 0, 0))
    for direction in (0, 1):
        go(z_copy(direction, 0, 1))
    go(x_copy(0, B, 0))
    go(c_copy(0, 0, A, 0))
    go(c_copy(0, 0, B, 1))

    rbuf[:, 0, 320:384, :] = jnp.zeros((32, 64, 256), BF)
    rbuf[:, 1, 256:320, :] = jnp.zeros((32, 64, 256), BF)

    def right_step(step, tail):
        @pl.when(step + 1 < 20)
        def _():
            p_copy(step + 1).start()

        p_copy(step).wait()
        here = step % 2
        for pairs in range(KB // 2):
            first, second = [], []
            for kk in (2 * pairs, 2 * pairs + 1):
                v = norm_lanes(pbuf[here, kk], gain).astype(BF)
                main, rest = v[0:64], v[64:80]
                first += [main, rest, rest, rest, rest]
                second += [rest, rest, rest, rest, main]
            for par, rows in ((0, first), (1, second)):
                v = dot_nt(wbt[par * 128:(par + 1) * 128, :], jnp.concatenate(rows, axis=0))
                v = sigmoid(v[64:]) * v[:64]
                for half in (0, 1):
                    tr[pl.ds(par * 1024 + 2 * pairs + half, 64, stride=KB), :] = v[:, half * 128:(half + 1) * 128]
        for par in (0, 1):
            v = tr[par * 1024:(par + 1) * 1024, :].astype(BF).reshape(32, 2, KB, 128)
            base = pl.multiple_of(step * KB, KB)
            for i in (0, 1):
                where = base + 64 if (tail and i == 1) else base
                rbuf[:, i, pl.ds(pl.multiple_of(where, KB), KB), par * 128:(par + 1) * 128] = v[:, i]

    def right_steps(lo, hi, tail=False):
        @pl.loop(lo, hi)
        def _(step):
            right_step(step, tail)

    right_steps(0, 4)
    x_arrival(0, A, 8).wait_recv()
    for direction in (0, 1):
        go(z_copy(direction, 0, 2))
    go(c_copy(1, 0, A, 0))
    right_steps(4, 8)
    serve(0, 0)
    right_steps(8, 12)
    serve_x(0)
    right_steps(12, 16)
    serve(0, 2)
    serve(0, 1)
    right_steps(16, 20, True)

    def contract(chips, half):
        @pl.loop(8 * half, 8 * half + 8)
        def _(o):
            tails = [[None, None] for _ in chips]
            for m in range(4):
                q, i = o * 2 + m // 2, m % 2
                lhs = []
                for lane_tile in range(3):
                    start = 64 if lane_tile == 2 else 32 * lane_tile + 16 * i
                    lhs.append(jnp.concatenate(
                        [lbuf[slot(cx, cz, cc), q, start:start + 16, :] for cx, cz in chips for cc in (0, 1)], axis=0))
                res = jnp.dot(jnp.concatenate(lhs, axis=1), rbuf[q, i], preferred_element_type=F32)
                for ci, (cx, cz) in enumerate(chips):
                    both = []
                    for cc in (0, 1):
                        base = (ci * 2 + cc) * 16
                        even = res[base:base + 8, 0:128]
                        odd = res[base + 8:base + 16, 128:256]
                        both.append(jnp.where(lane < 64, even, odd))
                        mix = jnp.where(lane < 64, odd, even)
                        old = tails[ci][cc]
                        tails[ci][cc] = mix if old is None else jnp.where((lane % 64) // 16 == m, mix, old)
                    sbuf[cx * 8 + cz, o, 16 * m:16 * m + 16, :] = jnp.concatenate(both, axis=0).astype(BF)
            for ci, (cx, cz) in enumerate(chips):
                sbuf[cx * 8 + cz, o, 64:80, :] = jnp.concatenate(tails[ci], axis=0).astype(BF)

    def y_copy(cx, cz, half):
        target = cx * 2 + cz // 4
        rel = (y + 4 - target) % 4
        octets = pl.ds(8 * half, 8)
        return target, pltpu.make_async_remote_copy(
            src_ref=sbuf.at[cx * 8 + cz, octets], dst_ref=ybuf.at[rel, cz % 4, octets],
            send_sem=ys.at[cx * 8 + cz, half], recv_sem=yr.at[rel, cz % 4, half],
            device_id=dev(target, xh, x, z, c), device_id_type=MESH)

    def send_sums(cx, cz, half):
        target, copy = y_copy(cx, cz, half)

        @pl.when(target != y)
        def _():
            copy.start()

    def group(offsets, half):
        for o in offsets:
            have(o, half)
        chips = [(cx, at(o)) for o in offsets for cx in (0, 1)]
        contract(chips, half)
        for cx, cz in chips:
            send_sums(cx, cz, half)

    def total(zi, o):
        v = sbuf[(y // 2) * 8 + (y % 2) * 4 + zi, o].astype(F32)
        for rel in (1, 2, 3):
            v += ybuf[rel, zi, o].astype(F32)
        return v

    def h_copy(zz, half):
        octets = pl.ds(8 * half, 8)
        return pltpu.make_async_remote_copy(
            src_ref=xhs.at[zz, octets], dst_ref=xhr.at[zz, octets], send_sem=hs.at[zz, half],
            recv_sem=hr.at[zz, half], device_id=twin, device_id_type=MESH)

    def collect(offsets, half):
        for off in offsets:
            cz = at(off)
            zi = cz % 4
            zz = zi % 2

            @pl.when(cz // 4 == y % 2)
            def _():
                for rel in (1, 2, 3):
                    octets = pl.ds(8 * half, 8)
                    pltpu.make_async_remote_copy(
                        src_ref=ybuf.at[rel, zi, octets], dst_ref=ybuf.at[rel, zi, octets],
                        send_sem=ys.at[0, half], recv_sem=yr.at[rel, zi, half],
                        device_id=twin, device_id_type=MESH).wait_recv()

                @pl.when(zi // 2 == xh)
                def _():
                    @pl.loop(8 * half, 8 * half + 8, unroll=2)
                    def _(o):
                        fbuf[zz, o] = total(zi, o)

                @pl.when(zi // 2 != xh)
                def _():
                    @pl.loop(8 * half, 8 * half + 8, unroll=2)
                    def _(o):
                        xhs[zz, o] = total(zi, o).astype(BF)

                    h_copy(zz, half).start()

    def make_gates():
        for copy in g_copies:
            copy.wait()

        @pl.loop(0, 32, unroll=4)
        def _(i):
            v = norm_lanes(gwin[i // 8, i % 8], gain).astype(BF)
            gates[i] = sigmoid(jnp.dot(v, g_w[...], preferred_element_type=F32))

    def finish(zz):
        for half in (0, 1):
            h_copy(zz, half).wait_recv()

        @pl.loop(0, 16, unroll=2)
        def _(o):
            v = fbuf[zz, o] + xhr[zz, o].astype(F32)
            rest = v[64:80]
            for m in range(4):
                main = v[16 * m:16 * m + 16]
                even = jnp.where(lane16 < 64, main, pltpu.roll(rest, (128 - 16 * m) % 128, 1))
                odd = jnp.where(lane16 < 64, pltpu.roll(main, 64, 1), pltpu.roll(rest, 64 - 16 * m, 1))
                base = (o * 8 + 2 * m) * 16
                ubuf[pl.ds(pl.multiple_of(base, 16), 16), :] = even
                ubuf[pl.ds(pl.multiple_of(base + 16, 16), 16), :] = odd

        @pl.loop(0, 16, unroll=4)
        def _(r):
            u = ubuf[pl.ds(r, 128, stride=16), :]
            u = u - jnp.mean(u, axis=0, keepdims=True)
            spread = jnp.mean(u * u, axis=0, keepdims=True)
            u = (u * lax.rsqrt(spread + EPS) * gain_col).T[0:80].astype(BF)
            v = jnp.dot(u, o_w[...], preferred_element_type=F32)
            out[zz * 16 + r] = (gates[zz * 16 + r] * v).astype(BF)

    gain_col = jnp.broadcast_to(out_gain[...], (128, 128)).T

    group([0], 0)
    group([0], 1)
    serve(1, 0)
    group([1, 7], 0)
    collect([0], 0)
    serve_x(1)
    serve_x(7)
    serve(1, 2)
    group([1, 7], 1)
    collect([0], 1)
    serve(1, 1)
    make_gates()
    serve(2, 0)
    group([2, 6], 0)
    collect([1, 7], 0)
    serve_x(2)
    serve_x(6)
    serve(2, 2)
    group([2, 6], 1)
    collect([1, 7], 1)
    serve(2, 1)
    serve(3, 0)
    group([3, 5], 0)
    serve_x(3)
    serve_x(5)
    serve(3, 1)
    group([3, 5], 1)
    collect([2, 6], 0)
    serve(3, 2)
    group([4], 0)
    serve_x(4)
    group([4], 1)
    collect([2, 6], 1)
    collect([3, 5], 0)
    collect([3, 5], 1)

    place = (z + 8 - ((y % 2) * 4 + xh * 2)) % 8
    far = jnp.where((place >= 1) & (place <= 4), 0, 1)
    finish(1 - far)
    collect([4], 0)
    collect([4], 1)
    finish(far)

    for copy in sent:
        copy.wait_send()
    for half in (0, 1):
        for zz in (0, 1):
            h_copy(zz, half).wait_send()
        for cx in (0, 1):
            for o in range(8):
                target, copy = y_copy(cx, at(o), half)

                @pl.when(target != y)
                def _():
                    copy.wait_send()


def step(pair, in_gain, a_w, b_w, g_w, out_gain, o_w):
    vmem = pl.BlockSpec(memory_space=pltpu.VMEM)
    dma = pltpu.SemaphoreType.DMA
    return pl.pallas_call(
        kernel,
        out_shape=jax.ShapeDtypeStruct((32, 80, 128), BF),
        in_specs=[pl.BlockSpec(memory_space=pl.ANY)] + [vmem] * 6,
        out_specs=vmem,
        scratch_shapes=[
            pltpu.VMEM((320, 16, 128), BF),
            pltpu.VMEM((2, KB, 80, 128), BF),
            pltpu.VMEM((4, 8, 80, 128), BF),
            pltpu.VMEM((256, 128), BF),
            pltpu.VMEM((256, 128), BF),
            pltpu.VMEM((3072, 128), F32),
            pltpu.VMEM((3072, 128), F32),
            pltpu.VMEM((2048, 128), F32),
            pltpu.VMEM((32, 32, 80, 128), BF),
            pltpu.VMEM((32, 2, 384, 256), BF),
            pltpu.VMEM((16, 16, 80, 128), BF),
            pltpu.VMEM((4, 4, 16, 80, 128), BF),
            pltpu.VMEM((2, 16, 80, 128), BF),
            pltpu.VMEM((2, 16, 80, 128), BF),
            pltpu.VMEM((2, 16, 80, 128), F32),
            pltpu.VMEM((2048, 128), F32),
            pltpu.VMEM((32, 80, 128), F32),
            dma, dma((2,)), dma((4,)),
            dma((2, 4, 3)), dma((2, 4, 3)),
            dma((9,)), dma((9,)),
            dma((2, 8, 3)), dma((2, 8, 3)),
            dma((16, 2)), dma((4, 4, 2)),
            dma((2, 2)), dma((2, 2)),
        ],
        compiler_params=pltpu.CompilerParams(
            collective_id=0, has_side_effects=True, vmem_limit_bytes=63 * 2 ** 20),
        name="triangle",
    )(pair, in_gain.reshape(1, 128), a_w, b_w, g_w, out_gain.reshape(1, 128), o_w)


def solution(mesh):
    in_specs = (P("row", "col", None), P(), P(), P(), P(), P(), P())
    return jax.shard_map(step, mesh=mesh, in_specs=in_specs, out_specs=P("row", "col", None), check_vma=False)
```

```python
import functools

import jax
import jax.numpy as jnp
from jax import lax
from jax.experimental import pallas as pl
from jax.experimental.pallas import tpu as pltpu
from jax.sharding import PartitionSpec as P

MESH = pl.DeviceIdType.MESH
BF = jnp.bfloat16
F32 = jnp.float32
EPS = 1e-05
KB = 16


def sigmoid(v):
    return 0.5 * jnp.tanh(0.5 * v) + 0.5


def norm_lanes(v, gain):
    f = v.astype(F32)
    f = f - jnp.mean(f, axis=-1, keepdims=True)
    spread = jnp.mean(f * f, axis=-1, keepdims=True)
    return f * lax.rsqrt(spread + EPS) * gain


def dot_nt(a, b):
    return lax.dot_general(a, b, (((1,), (1,)), ((), ())), preferred_element_type=F32)


def kernel(pair, in_gain, a_w, b_w, g_w, out_gain, o_w, out,
           win, pbuf, gwin, wat, wbt, t1, t2, tr, lbuf, rbuf, sbuf, ybuf, xhs, xhr, fbuf, ubuf, gates,
           win_sem, p_sem, g_sem, zs, zr, xs_, xr, cs, cr, ys, yr, hs, hr):
    row = lax.axis_index("row")
    col = lax.axis_index("col")
    y, xh = row // 2, row % 2
    x, z, c = col // 16, (col // 2) % 8, col % 2

    def dev(y_, xh_, x_, z_, c_):
        return (y_ * 2 + xh_, (x_ * 8 + z_) * 2 + c_)

    up = dev(y, xh, x, (z + 1) % 8, c)
    down = dev(y, xh, x, (z + 7) % 8, c)
    across = dev(y, xh, 1 - x, z, c)
    mate = dev(y, xh, x, z, 1 - c)
    twin = dev(y, 1 - xh, x, z, c)
    others = [dev((y + d) % 4, xh, x, z, c) for d in (1, 2, 3)]

    win_copy = pltpu.make_async_copy(pair.at[:, 0:16, :], win, win_sem)
    win_copy.start()

    def p_copy(step):
        slot = step % 2
        return pltpu.make_async_copy(pair.at[pl.ds(step * KB, KB)], pbuf.at[slot], p_sem.at[slot])

    p_copy(0).start()
    g_copies = [pltpu.make_async_copy(pair.at[80 * b:80 * b + 8], gwin.at[b], g_sem.at[b]) for b in range(4)]
    for copy in g_copies:
        copy.start()

    barrier = pltpu.get_barrier_semaphore()
    for d in [up, down, across, mate, twin] + others:
        pl.semaphore_signal(barrier, inc=1, device_id=d, device_id_type=MESH)

    lane = lax.broadcasted_iota(jnp.int32, (8, 128), 1)
    lane16 = lax.broadcasted_iota(jnp.int32, (16, 128), 1)
    gain = in_gain[...]

    wat[...] = a_w[...].astype(F32).T.astype(BF)
    t2[0:256, :] = b_w[...].astype(F32).T
    wbt[0:128, :] = t2[pl.ds(0, 128, stride=2), :].astype(BF)
    wbt[128:256, :] = t2[pl.ds(1, 128, stride=2), :].astype(BF)

    win_copy.wait()

    @pl.loop(0, 10, unroll=2)
    def _(i):
        v = win[pl.ds(i * 32, 32)].astype(F32)[:, 0:8, :]
        t1[pl.ds(pl.multiple_of(i * 256, 256), 256), :] = norm_lanes(v, gain).reshape(256, 128)

    t1[2560:3072, :] = jnp.zeros((512, 128), F32)
    def slot(x_, z_, c_):
        return (x_ * 8 + z_) * 2 + c_

    mine = slot(x, z, c)

    def left_half(half):
        h0 = half * 64
        weights = jnp.concatenate([wat[h0:h0 + 64, :], wat[128 + h0:192 + h0, :]], axis=0)
        for w in range(8):
            xw = t1[pl.ds(w, 384, stride=8), :].astype(BF)
            v = dot_nt(weights, xw)
            v = sigmoid(v[64:]) * v[:64]
            for t in range(3):
                t2[pl.ds(1024 * t + 8 * h0 + w, 64, stride=8), :] = v[:, t * 128:(t + 1) * 128]

        @pl.loop(half * 16, half * 16 + 16, unroll=4)
        def _(q):
            base = pl.multiple_of(q * 32, 32)
            lbuf[mine, q, 0:32, :] = t2[pl.ds(base, 32), :].astype(BF)
            lbuf[mine, q, 32:64, :] = t2[pl.ds(1024 + base, 32), :].astype(BF)
            low = t2[pl.ds(2048 + base, 16), :]
            high = pltpu.roll(t2[pl.ds(2048 + base + 16, 16), :], 64, 1)
            lbuf[mine, q, 64:80, :] = jnp.where(lane16 < 64, low, high).astype(BF)

    A, B = (0, 16), (16, 16)
    AU, AD, BU, BD = (0, 8), (8, 8), (16, 8), (24, 8)

    def part(x_, z_, c_, piece):
        return lbuf.at[slot(x_, z_, c_), pl.ds(piece[0], piece[1])]

    def z_piece(direction, n, k):
        if n < 3:
            return B if k == 1 else A
        return ((BU, BD) if k == 1 else (AU, AD))[direction]

    def z_copy(direction, n, k):
        origin = (z + 8 - n) % 8 if direction == 0 else (z + n) % 8
        ref = part(1 - x if k == 2 else x, origin, c, z_piece(direction, n, k))
        return pltpu.make_async_remote_copy(
            src_ref=ref, dst_ref=ref, send_sem=zs.at[direction, n, k], recv_sem=zr.at[direction, n, k],
            device_id=up if direction == 0 else down, device_id_type=MESH)

    def z_arrival(direction, n, k):
        origin = (z + 8 - (n + 1)) % 8 if direction == 0 else (z + n + 1) % 8
        ref = part(1 - x if k == 2 else x, origin, c, z_piece(direction, n, k))
        return pltpu.make_async_remote_copy(
            src_ref=ref, dst_ref=ref, send_sem=zs.at[direction, n, k], recv_sem=zr.at[direction, n, k],
            device_id=up if direction == 0 else down, device_id_type=MESH)

    def at(o):
        return (z + o) % 8

    def x_copy(o, piece, k):
        ref = part(x, at(o), c, piece)
        return pltpu.make_async_remote_copy(
            src_ref=ref, dst_ref=ref, send_sem=xs_.at[k], recv_sem=xr.at[k], device_id=across, device_id_type=MESH)

    def x_arrival(o, piece, k):
        ref = part(1 - x, at(o), c, piece)
        return pltpu.make_async_remote_copy(
            src_ref=ref, dst_ref=ref, send_sem=xs_.at[k], recv_sem=xr.at[k], device_id=across, device_id_type=MESH)

    def c_copy(side, o, piece, k):
        ref = part(x if side == 0 else 1 - x, at(o), c, piece)
        return pltpu.make_async_remote_copy(
            src_ref=ref, dst_ref=ref, send_sem=cs.at[side, o, k], recv_sem=cr.at[side, o, k],
            device_id=mate, device_id_type=MESH)

    def c_arrival(side, o, piece, k):
        ref = part(x if side == 0 else 1 - x, at(o), 1 - c, piece)
        return pltpu.make_async_remote_copy(
            src_ref=ref, dst_ref=ref, send_sem=cs.at[side, o, k], recv_sem=cr.at[side, o, k],
            device_id=mate, device_id_type=MESH)

    sent = []

    def go(copy):
        copy.start()
        sent.append(copy)

    def c_pieces(o):
        if o == 4:
            return [(AU, 0), (AD, 2), (BU, 1), (BD, 3)]
        return [(A, 0), (B, 1)]

    def serve(n, k):
        for direction in (0, 1):
            z_arrival(direction, n, k).wait_recv()
            if n < 3:
                go(z_copy(direction, n + 1, k))
            o = (8 - (n + 1)) % 8 if direction == 0 else n + 1
            piece = z_piece(direction, n, k)
            second = 2 if n == 3 and direction == 1 else 0
            if k == 1:
                go(x_copy(o, piece, 9 if second else o))
            go(c_copy(1 if k == 2 else 0, o, piece, second + (1 if k == 1 else 0)))

    def serve_x(o):
        for piece, k in c_pieces(o):
            if k % 2 == 1:
                x_arrival(o, piece, 9 if k == 3 else o).wait_recv()
                go(c_copy(1, o, piece, k))

    def have(o, half):
        for side in (0, 1):
            for piece, k in c_pieces(o):
                if k % 2 == half:
                    c_arrival(side, o, piece, k).wait_recv()

    left_half(1)
    pl.semaphore_wait(barrier, 8)
    for direction in (0, 1):
        go(z_copy(direction, 0, 1))
    go(c_copy(0, 0, B, 1))
    left_half(0)
    go(x_copy(0, A, 8))
    for direction in (0, 1):
        go(z_copy(direction, 0, 0))
    go(x_copy(0, B, 0))
    go(c_copy(0, 0, A, 0))

    rbuf[:, 0, 320:384, :] = jnp.zeros((32, 64, 256), BF)
    rbuf[:, 1, 256:320, :] = jnp.zeros((32, 64, 256), BF)

    def right_step(step, tail):
        @pl.when(step + 1 < 20)
        def _():
            p_copy(step + 1).start()

        p_copy(step).wait()
        here = step % 2
        for pairs in range(KB // 2):
            first, second = [], []
            for kk in (2 * pairs, 2 * pairs + 1):
                v = norm_lanes(pbuf[here, kk], gain).astype(BF)
                main, rest = v[0:64], v[64:80]
                first += [main, rest, rest, rest, rest]
                second += [rest, rest, rest, rest, main]
            for par, rows in ((0, first), (1, second)):
                v = dot_nt(wbt[par * 128:(par + 1) * 128, :], jnp.concatenate(rows, axis=0))
                v = sigmoid(v[64:]) * v[:64]
                for half in (0, 1):
                    tr[pl.ds(par * 1024 + 2 * pairs + half, 64, stride=KB), :] = v[:, half * 128:(half + 1) * 128]
        for par in (0, 1):
            v = tr[par * 1024:(par + 1) * 1024, :].astype(BF).reshape(32, 2, KB, 128)
            base = pl.multiple_of(step * KB, KB)
            for i in (0, 1):
                where = base + 64 if (tail and i == 1) else base
                rbuf[:, i, pl.ds(pl.multiple_of(where, KB), KB), par * 128:(par + 1) * 128] = v[:, i]

    def right_steps(lo, hi, tail=False):
        @pl.loop(lo, hi)
        def _(step):
            right_step(step, tail)

    right_steps(0, 4)
    x_arrival(0, A, 8).wait_recv()
    for direction in (0, 1):
        go(z_copy(direction, 0, 2))
    go(c_copy(1, 0, A, 0))
    serve(0, 1)
    right_steps(4, 9)
    serve_x(0)
    serve(0, 0)
    right_steps(9, 13)
    serve_x(1)
    serve_x(7)
    serve(0, 2)
    right_steps(13, 16)
    right_steps(16, 20, True)

    def contract(chips, half):
        @pl.loop(8 * half, 8 * half + 8)
        def _(o):
            tails = [[None, None] for _ in chips]
            for m in range(4):
                q, i = o * 2 + m // 2, m % 2
                lhs = []
                for lane_tile in range(3):
                    start = 64 if lane_tile == 2 else 32 * lane_tile + 16 * i
                    lhs.append(jnp.concatenate(
                        [lbuf[slot(cx, cz, cc), q, start:start + 16, :] for cx, cz in chips for cc in (0, 1)], axis=0))
                res = jnp.dot(jnp.concatenate(lhs, axis=1), rbuf[q, i], preferred_element_type=F32)
                for ci, (cx, cz) in enumerate(chips):
                    both = []
                    for cc in (0, 1):
                        base = (ci * 2 + cc) * 16
                        even = res[base:base + 8, 0:128]
                        odd = res[base + 8:base + 16, 128:256]
                        both.append(jnp.where(lane < 64, even, odd))
                        mix = jnp.where(lane < 64, odd, even)
                        old = tails[ci][cc]
                        tails[ci][cc] = mix if old is None else jnp.where((lane % 64) // 16 == m, mix, old)
                    sbuf[cx * 8 + cz, o, 16 * m:16 * m + 16, :] = jnp.concatenate(both, axis=0).astype(BF)
            for ci, (cx, cz) in enumerate(chips):
                sbuf[cx * 8 + cz, o, 64:80, :] = jnp.concatenate(tails[ci], axis=0).astype(BF)

    def y_copy(cx, cz, half):
        target = cx * 2 + cz // 4
        rel = (y + 4 - target) % 4
        octets = pl.ds(8 * half, 8)
        return target, rel, pltpu.make_async_remote_copy(
            src_ref=sbuf.at[cx * 8 + cz, octets], dst_ref=ybuf.at[rel, cz % 4, octets],
            send_sem=ys.at[cx * 8 + cz, half], recv_sem=yr.at[rel, cz % 4, half],
            device_id=dev((target + jnp.where(rel == 2, 1 + 2 * c, 0)) % 4, xh, x, z, c), device_id_type=MESH)

    def send_sums(cx, cz, half):
        target, rel, copy = y_copy(cx, cz, half)

        @pl.when((rel != 0) & (rel != 1 + 2 * c))
        def _():
            copy.start()

    def y_come(rel, zi, half):
        ref = ybuf.at[rel, zi, pl.ds(8 * half, 8)]
        pltpu.make_async_remote_copy(
            src_ref=ref, dst_ref=ref, send_sem=ys.at[0, half], recv_sem=yr.at[rel, zi, half],
            device_id=twin, device_id_type=MESH).wait_recv()

    def relay(offsets, half):
        for o in offsets:
            for cx in (0, 1):
                cz = at(o)
                target, rel, copy = y_copy(cx, cz, half)

                @pl.when(rel == 1 + 2 * c)
                def _():
                    zi = cz % 4
                    mid = cx * 8 + cz
                    y_come(2, zi, half)

                    @pl.loop(8 * half, 8 * half + 8, unroll=2)
                    def _(k):
                        sbuf[mid, k] = (sbuf[mid, k].astype(F32) + ybuf[2, zi, k].astype(F32)).astype(BF)

                    copy.start()

    def group(offsets, half):
        for o in offsets:
            have(o, half)
        chips = [(cx, at(o)) for o in offsets for cx in (0, 1)]
        contract(chips, half)
        for cx, cz in chips:
            send_sums(cx, cz, half)

    def total(zi, o):
        v = sbuf[(y // 2) * 8 + (y % 2) * 4 + zi, o].astype(F32)
        for rel in (1, 3):
            v += ybuf[rel, zi, o].astype(F32)
        return v

    def h_copy(zz, half):
        octets = pl.ds(8 * half, 8)
        return pltpu.make_async_remote_copy(
            src_ref=xhs.at[zz, octets], dst_ref=xhr.at[zz, octets], send_sem=hs.at[zz, half],
            recv_sem=hr.at[zz, half], device_id=twin, device_id_type=MESH)

    def collect(offsets, half):
        for off in offsets:
            cz = at(off)
            zi = cz % 4
            zz = zi % 2

            @pl.when(cz // 4 == y % 2)
            def _():
                for rel in (1, 3):
                    y_come(rel, zi, half)

                @pl.when(zi // 2 == xh)
                def _():
                    @pl.loop(8 * half, 8 * half + 8, unroll=2)
                    def _(o):
                        fbuf[zz, o] = total(zi, o)

                @pl.when(zi // 2 != xh)
                def _():
                    @pl.loop(8 * half, 8 * half + 8, unroll=2)
                    def _(o):
                        xhs[zz, o] = total(zi, o).astype(BF)

                    h_copy(zz, half).start()

    def make_gates():
        for copy in g_copies:
            copy.wait()

        @pl.loop(0, 32, unroll=4)
        def _(i):
            v = norm_lanes(gwin[i // 8, i % 8], gain).astype(BF)
            gates[i] = sigmoid(jnp.dot(v, g_w[...], preferred_element_type=F32))

    def finish(zz):
        for half in (0, 1):
            h_copy(zz, half).wait_recv()

        @pl.loop(0, 16, unroll=2)
        def _(o):
            v = fbuf[zz, o] + xhr[zz, o].astype(F32)
            rest = v[64:80]
            for m in range(4):
                main = v[16 * m:16 * m + 16]
                even = jnp.where(lane16 < 64, main, pltpu.roll(rest, (128 - 16 * m) % 128, 1))
                odd = jnp.where(lane16 < 64, pltpu.roll(main, 64, 1), pltpu.roll(rest, 64 - 16 * m, 1))
                base = (o * 8 + 2 * m) * 16
                ubuf[pl.ds(pl.multiple_of(base, 16), 16), :] = even
                ubuf[pl.ds(pl.multiple_of(base + 16, 16), 16), :] = odd

        @pl.loop(0, 16, unroll=4)
        def _(r):
            u = ubuf[pl.ds(r, 128, stride=16), :]
            u = u - jnp.mean(u, axis=0, keepdims=True)
            spread = jnp.mean(u * u, axis=0, keepdims=True)
            u = (u * lax.rsqrt(spread + EPS) * gain_col).T[0:80].astype(BF)
            v = jnp.dot(u, o_w[...], preferred_element_type=F32)
            out[zz * 16 + r] = (gates[zz * 16 + r] * v).astype(BF)

    gain_col = jnp.broadcast_to(out_gain[...], (128, 128)).T

    group([0], 1)
    group([0], 0)
    serve(1, 1)
    relay([0], 1)
    relay([0], 0)
    group([1, 7], 1)
    serve(1, 0)
    group([1, 7], 0)
    serve(1, 2)
    relay([1, 7], 1)
    serve_x(2)
    serve_x(6)
    relay([1, 7], 0)
    collect([0], 1)
    collect([0], 0)
    group([2, 6], 1)
    serve(2, 1)
    group([2, 6], 0)
    serve(2, 0)
    make_gates()
    relay([2, 6], 1)
    relay([2, 6], 0)
    collect([1, 7], 1)
    collect([1, 7], 0)
    serve(2, 2)
    serve_x(3)
    serve_x(5)
    group([3, 5], 1)
    serve(3, 1)
    group([3, 5], 0)
    relay([3, 5], 1)
    collect([2, 6], 1)
    serve(3, 0)
    serve(3, 2)
    relay([3, 5], 0)
    serve_x(4)
    group([4], 0)
    group([4], 1)
    collect([2, 6], 0)
    relay([4], 0)
    relay([4], 1)
    collect([3, 5], 1)
    collect([3, 5], 0)

    place = (z + 8 - ((y % 2) * 4 + xh * 2)) % 8
    far = jnp.where((place >= 1) & (place <= 4), 0, 1)
    finish(1 - far)
    collect([4], 0)
    collect([4], 1)
    finish(far)

    for copy in sent:
        copy.wait_send()
    for half in (0, 1):
        for zz in (0, 1):
            h_copy(zz, half).wait_send()
        for cx in (0, 1):
            for o in range(8):
                target, rel, copy = y_copy(cx, at(o), half)

                @pl.when(target != y)
                def _():
                    copy.wait_send()


def step(pair, in_gain, a_w, b_w, g_w, out_gain, o_w):
    vmem = pl.BlockSpec(memory_space=pltpu.VMEM)
    dma = pltpu.SemaphoreType.DMA
    return pl.pallas_call(
        kernel,
        out_shape=jax.ShapeDtypeStruct((32, 80, 128), BF),
        in_specs=[pl.BlockSpec(memory_space=pl.ANY)] + [vmem] * 6,
        out_specs=vmem,
        scratch_shapes=[
            pltpu.VMEM((320, 16, 128), BF),
            pltpu.VMEM((2, KB, 80, 128), BF),
            pltpu.VMEM((4, 8, 80, 128), BF),
            pltpu.VMEM((256, 128), BF),
            pltpu.VMEM((256, 128), BF),
            pltpu.VMEM((3072, 128), F32),
            pltpu.VMEM((3072, 128), F32),
            pltpu.VMEM((2048, 128), F32),
            pltpu.VMEM((32, 32, 80, 128), BF),
            pltpu.VMEM((32, 2, 384, 256), BF),
            pltpu.VMEM((16, 16, 80, 128), BF),
            pltpu.VMEM((4, 4, 16, 80, 128), BF),
            pltpu.VMEM((2, 16, 80, 128), BF),
            pltpu.VMEM((2, 16, 80, 128), BF),
            pltpu.VMEM((2, 16, 80, 128), F32),
            pltpu.VMEM((2048, 128), F32),
            pltpu.VMEM((32, 80, 128), F32),
            dma, dma((2,)), dma((4,)),
            dma((2, 4, 3)), dma((2, 4, 3)),
            dma((10,)), dma((10,)),
            dma((2, 8, 4)), dma((2, 8, 4)),
            dma((16, 2)), dma((4, 4, 2)),
            dma((2, 2)), dma((2, 2)),
        ],
        compiler_params=pltpu.CompilerParams(
            collective_id=0, has_side_effects=True, vmem_limit_bytes=63 * 2 ** 20),
        name="triangle",
    )(pair, in_gain.reshape(1, 128), a_w, b_w, g_w, out_gain.reshape(1, 128), o_w)


def solution(mesh):
    in_specs = (P("row", "col", None), P(), P(), P(), P(), P(), P())
    return jax.shard_map(step, mesh=mesh, in_specs=in_specs, out_specs=P("row", "col", None), check_vma=False)
```

```python
import functools

import jax
import jax.numpy as jnp
from jax import lax
from jax.experimental import pallas as pl
from jax.experimental.pallas import tpu as pltpu
from jax.sharding import PartitionSpec as P

MESH = pl.DeviceIdType.MESH
BF = jnp.bfloat16
F32 = jnp.float32
EPS = 1e-05
KB = 16


def sigmoid(v):
    return 0.5 * jnp.tanh(0.5 * v) + 0.5


def norm_lanes(v, gain):
    f = v.astype(F32)
    f = f - jnp.mean(f, axis=-1, keepdims=True)
    spread = jnp.mean(f * f, axis=-1, keepdims=True)
    return f * lax.rsqrt(spread + EPS) * gain


def dot_nt(a, b):
    return lax.dot_general(a, b, (((1,), (1,)), ((), ())), preferred_element_type=F32)


def kernel(pair, in_gain, a_w, b_w, g_w, out_gain, o_w, out,
           win, pbuf, gwin, wat, wbt, t1, t2, tr, lbuf, rbuf, sbuf, ybuf, xhs, xhr, fbuf, ubuf, gates,
           win_sem, p_sem, g_sem, zs, zr, xs_, xr, cs, cr, ys, yr, hs, hr):
    row = lax.axis_index("row")
    col = lax.axis_index("col")
    y, xh = row // 2, row % 2
    x, z, c = col // 16, (col // 2) % 8, col % 2

    def dev(y_, xh_, x_, z_, c_):
        return (y_ * 2 + xh_, (x_ * 8 + z_) * 2 + c_)

    up = dev(y, xh, x, (z + 1) % 8, c)
    down = dev(y, xh, x, (z + 7) % 8, c)
    across = dev(y, xh, 1 - x, z, c)
    mate = dev(y, xh, x, z, 1 - c)
    twin = dev(y, 1 - xh, x, z, c)
    others = [dev((y + d) % 4, xh, x, z, c) for d in (1, 2, 3)]

    win_copy = pltpu.make_async_copy(pair.at[:, 0:16, :], win, win_sem)
    win_copy.start()

    def p_copy(step):
        slot = step % 2
        return pltpu.make_async_copy(pair.at[pl.ds(step * KB, KB)], pbuf.at[slot], p_sem.at[slot])

    p_copy(0).start()
    g_copies = [pltpu.make_async_copy(pair.at[80 * b:80 * b + 8], gwin.at[b], g_sem.at[b]) for b in range(4)]
    for copy in g_copies:
        copy.start()

    barrier = pltpu.get_barrier_semaphore()
    for d in [up, down, across, mate, twin] + others:
        pl.semaphore_signal(barrier, inc=1, device_id=d, device_id_type=MESH)

    lane = lax.broadcasted_iota(jnp.int32, (8, 128), 1)
    lane16 = lax.broadcasted_iota(jnp.int32, (16, 128), 1)
    gain = in_gain[...]

    wat[...] = a_w[...].astype(F32).T.astype(BF)
    t2[0:256, :] = b_w[...].astype(F32).T
    wbt[0:128, :] = t2[pl.ds(0, 128, stride=2), :].astype(BF)
    wbt[128:256, :] = t2[pl.ds(1, 128, stride=2), :].astype(BF)

    win_copy.wait()

    @pl.loop(0, 10, unroll=2)
    def _(i):
        v = win[pl.ds(i * 32, 32)].astype(F32)[:, 0:8, :]
        t1[pl.ds(pl.multiple_of(i * 256, 256), 256), :] = norm_lanes(v, gain).reshape(256, 128)

    t1[2560:3072, :] = jnp.zeros((512, 128), F32)
    def slot(x_, z_, c_):
        return (x_ * 8 + z_) * 2 + c_

    mine = slot(x, z, c)

    def left_half(half):
        h0 = half * 64
        weights = jnp.concatenate([wat[h0:h0 + 64, :], wat[128 + h0:192 + h0, :]], axis=0)
        for w in range(8):
            xw = t1[pl.ds(w, 384, stride=8), :].astype(BF)
            v = dot_nt(weights, xw)
            v = sigmoid(v[64:]) * v[:64]
            for t in range(3):
                t2[pl.ds(1024 * t + 8 * h0 + w, 64, stride=8), :] = v[:, t * 128:(t + 1) * 128]

        @pl.loop(half * 16, half * 16 + 16, unroll=4)
        def _(q):
            base = pl.multiple_of(q * 32, 32)
            lbuf[mine, q, 0:32, :] = t2[pl.ds(base, 32), :].astype(BF)
            lbuf[mine, q, 32:64, :] = t2[pl.ds(1024 + base, 32), :].astype(BF)
            low = t2[pl.ds(2048 + base, 16), :]
            high = pltpu.roll(t2[pl.ds(2048 + base + 16, 16), :], 64, 1)
            lbuf[mine, q, 64:80, :] = jnp.where(lane16 < 64, low, high).astype(BF)

    A, B = (0, 16), (16, 16)
    AU, AD, BU, BD = (0, 8), (8, 8), (16, 8), (24, 8)

    def part(x_, z_, c_, piece):
        return lbuf.at[slot(x_, z_, c_), pl.ds(piece[0], piece[1])]

    def z_piece(direction, n, k):
        if n < 3:
            return B if k == 1 else A
        return ((BU, BD) if k == 1 else (AU, AD))[direction]

    def z_copy(direction, n, k):
        origin = (z + 8 - n) % 8 if direction == 0 else (z + n) % 8
        ref = part(1 - x if k == 2 else x, origin, c, z_piece(direction, n, k))
        return pltpu.make_async_remote_copy(
            src_ref=ref, dst_ref=ref, send_sem=zs.at[direction, n, k], recv_sem=zr.at[direction, n, k],
            device_id=up if direction == 0 else down, device_id_type=MESH)

    def z_arrival(direction, n, k):
        origin = (z + 8 - (n + 1)) % 8 if direction == 0 else (z + n + 1) % 8
        ref = part(1 - x if k == 2 else x, origin, c, z_piece(direction, n, k))
        return pltpu.make_async_remote_copy(
            src_ref=ref, dst_ref=ref, send_sem=zs.at[direction, n, k], recv_sem=zr.at[direction, n, k],
            device_id=up if direction == 0 else down, device_id_type=MESH)

    def at(o):
        return (z + o) % 8

    def x_copy(o, piece, k):
        ref = part(x, at(o), c, piece)
        return pltpu.make_async_remote_copy(
            src_ref=ref, dst_ref=ref, send_sem=xs_.at[k], recv_sem=xr.at[k], device_id=across, device_id_type=MESH)

    def x_arrival(o, piece, k):
        ref = part(1 - x, at(o), c, piece)
        return pltpu.make_async_remote_copy(
            src_ref=ref, dst_ref=ref, send_sem=xs_.at[k], recv_sem=xr.at[k], device_id=across, device_id_type=MESH)

    def c_copy(side, o, piece, k):
        ref = part(x if side == 0 else 1 - x, at(o), c, piece)
        return pltpu.make_async_remote_copy(
            src_ref=ref, dst_ref=ref, send_sem=cs.at[side, o, k], recv_sem=cr.at[side, o, k],
            device_id=mate, device_id_type=MESH)

    def c_arrival(side, o, piece, k):
        ref = part(x if side == 0 else 1 - x, at(o), 1 - c, piece)
        return pltpu.make_async_remote_copy(
            src_ref=ref, dst_ref=ref, send_sem=cs.at[side, o, k], recv_sem=cr.at[side, o, k],
            device_id=mate, device_id_type=MESH)

    sent = []

    def go(copy):
        copy.start()
        sent.append(copy)

    def c_pieces(o):
        if o == 4:
            return [(AU, 0), (AD, 2), (BU, 1), (BD, 3)]
        return [(A, 0), (B, 1)]

    def serve(n, k):
        for direction in (0, 1):
            z_arrival(direction, n, k).wait_recv()
            if n < 3:
                go(z_copy(direction, n + 1, k))
            o = (8 - (n + 1)) % 8 if direction == 0 else n + 1
            piece = z_piece(direction, n, k)
            second = 2 if n == 3 and direction == 1 else 0
            if k == 1:
                go(x_copy(o, piece, 9 if second else o))
            go(c_copy(1 if k == 2 else 0, o, piece, second + (1 if k == 1 else 0)))

    def serve_x(o):
        for piece, k in c_pieces(o):
            if k % 2 == 1:
                x_arrival(o, piece, 9 if k == 3 else o).wait_recv()
                go(c_copy(1, o, piece, k))

    def have(o, half):
        for side in (0, 1):
            for piece, k in c_pieces(o):
                if k % 2 == half:
                    c_arrival(side, o, piece, k).wait_recv()

    left_half(1)
    pl.semaphore_wait(barrier, 8)
    for direction in (0, 1):
        go(z_copy(direction, 0, 1))
    go(c_copy(0, 0, B, 1))
    left_half(0)
    go(x_copy(0, A, 8))
    for direction in (0, 1):
        go(z_copy(direction, 0, 0))
    go(x_copy(0, B, 0))
    go(c_copy(0, 0, A, 0))

    rbuf[:, 0, 320:384, :] = jnp.zeros((32, 64, 256), BF)
    rbuf[:, 1, 256:320, :] = jnp.zeros((32, 64, 256), BF)

    def right_step(step, tail):
        @pl.when(step + 1 < 20)
        def _():
            p_copy(step + 1).start()

        p_copy(step).wait()
        here = step % 2
        for pairs in range(KB // 2):
            first, second = [], []
            for kk in (2 * pairs, 2 * pairs + 1):
                v = norm_lanes(pbuf[here, kk], gain).astype(BF)
                main, rest = v[0:64], v[64:80]
                first += [main, rest, rest, rest, rest]
                second += [rest, rest, rest, rest, main]
            for par, rows in ((0, first), (1, second)):
                v = dot_nt(wbt[par * 128:(par + 1) * 128, :], jnp.concatenate(rows, axis=0))
                v = sigmoid(v[64:]) * v[:64]
                for half in (0, 1):
                    tr[pl.ds(par * 1024 + 2 * pairs + half, 64, stride=KB), :] = v[:, half * 128:(half + 1) * 128]
        for par in (0, 1):
            v = tr[par * 1024:(par + 1) * 1024, :].astype(BF).reshape(32, 2, KB, 128)
            base = pl.multiple_of(step * KB, KB)
            for i in (0, 1):
                where = base + 64 if (tail and i == 1) else base
                rbuf[:, i, pl.ds(pl.multiple_of(where, KB), KB), par * 128:(par + 1) * 128] = v[:, i]

    def right_steps(lo, hi, tail=False):
        @pl.loop(lo, hi)
        def _(step):
            right_step(step, tail)

    right_steps(0, 4)
    x_arrival(0, A, 8).wait_recv()
    for direction in (0, 1):
        go(z_copy(direction, 0, 2))
    go(c_copy(1, 0, A, 0))
    serve(0, 1)
    right_steps(4, 9)
    serve_x(0)
    serve(0, 0)
    right_steps(9, 13)
    serve_x(1)
    serve_x(7)
    serve(0, 2)
    right_steps(13, 16)
    right_steps(16, 20, True)

    def contract(chips, half):
        @pl.loop(8 * half, 8 * half + 8, unroll=2)
        def _(o):
            tails = [[None, None] for _ in chips]
            for m in range(4):
                q, i = o * 2 + m // 2, m % 2
                lhs = []
                for lane_tile in range(3):
                    start = 64 if lane_tile == 2 else 32 * lane_tile + 16 * i
                    lhs.append(jnp.concatenate(
                        [lbuf[slot(cx, cz, cc), q, start:start + 16, :] for cx, cz in chips for cc in (0, 1)], axis=0))
                res = jnp.dot(jnp.concatenate(lhs, axis=1), rbuf[q, i], preferred_element_type=F32)
                for ci, (cx, cz) in enumerate(chips):
                    both = []
                    for cc in (0, 1):
                        base = (ci * 2 + cc) * 16
                        even = res[base:base + 8, 0:128]
                        odd = res[base + 8:base + 16, 128:256]
                        both.append(jnp.where(lane < 64, even, odd))
                        mix = jnp.where(lane < 64, odd, even)
                        old = tails[ci][cc]
                        tails[ci][cc] = mix if old is None else jnp.where((lane % 64) // 16 == m, mix, old)
                    sbuf[cx * 8 + cz, o, 16 * m:16 * m + 16, :] = jnp.concatenate(both, axis=0).astype(BF)
            for ci, (cx, cz) in enumerate(chips):
                sbuf[cx * 8 + cz, o, 64:80, :] = jnp.concatenate(tails[ci], axis=0).astype(BF)

    def y_copy(cx, cz, half):
        target = cx * 2 + cz // 4
        rel = (y + 4 - target) % 4
        octets = pl.ds(8 * half, 8)
        return target, rel, pltpu.make_async_remote_copy(
            src_ref=sbuf.at[cx * 8 + cz, octets], dst_ref=ybuf.at[rel, cz % 4, octets],
            send_sem=ys.at[cx * 8 + cz, half], recv_sem=yr.at[rel, cz % 4, half],
            device_id=dev((target + jnp.where(rel == 2, 1 + 2 * c, 0)) % 4, xh, x, z, c), device_id_type=MESH)

    def send_sums(cx, cz, half):
        target, rel, copy = y_copy(cx, cz, half)

        @pl.when((rel != 0) & (rel != 1 + 2 * c))
        def _():
            copy.start()

    def y_come(rel, zi, half):
        ref = ybuf.at[rel, zi, pl.ds(8 * half, 8)]
        pltpu.make_async_remote_copy(
            src_ref=ref, dst_ref=ref, send_sem=ys.at[0, half], recv_sem=yr.at[rel, zi, half],
            device_id=twin, device_id_type=MESH).wait_recv()

    def relay(offsets, half):
        for o in offsets:
            for cx in (0, 1):
                cz = at(o)
                target, rel, copy = y_copy(cx, cz, half)

                @pl.when(rel == 1 + 2 * c)
                def _():
                    zi = cz % 4
                    mid = cx * 8 + cz
                    y_come(2, zi, half)

                    @pl.loop(8 * half, 8 * half + 8, unroll=2)
                    def _(k):
                        sbuf[mid, k] = (sbuf[mid, k].astype(F32) + ybuf[2, zi, k].astype(F32)).astype(BF)

                    copy.start()

    def group(offsets, half):
        for o in offsets:
            have(o, half)
        chips = [(cx, at(o)) for o in offsets for cx in (0, 1)]
        contract(chips, half)
        for cx, cz in chips:
            send_sums(cx, cz, half)

    def total(zi, o):
        v = sbuf[(y // 2) * 8 + (y % 2) * 4 + zi, o].astype(F32)
        for rel in (1, 3):
            v += ybuf[rel, zi, o].astype(F32)
        return v

    def h_copy(zz, half):
        octets = pl.ds(8 * half, 8)
        return pltpu.make_async_remote_copy(
            src_ref=xhs.at[zz, octets], dst_ref=xhr.at[zz, octets], send_sem=hs.at[zz, half],
            recv_sem=hr.at[zz, half], device_id=twin, device_id_type=MESH)

    def collect(offsets, half):
        for off in offsets:
            cz = at(off)
            zi = cz % 4
            zz = zi % 2

            @pl.when(cz // 4 == y % 2)
            def _():
                for rel in (1, 3):
                    y_come(rel, zi, half)

                @pl.when(zi // 2 == xh)
                def _():
                    @pl.loop(8 * half, 8 * half + 8, unroll=2)
                    def _(o):
                        fbuf[zz, o] = total(zi, o)

                @pl.when(zi // 2 != xh)
                def _():
                    @pl.loop(8 * half, 8 * half + 8, unroll=2)
                    def _(o):
                        xhs[zz, o] = total(zi, o).astype(BF)

                    h_copy(zz, half).start()

    def make_gates():
        for copy in g_copies:
            copy.wait()

        @pl.loop(0, 32, unroll=4)
        def _(i):
            v = norm_lanes(gwin[i // 8, i % 8], gain).astype(BF)
            gates[i] = sigmoid(jnp.dot(v, g_w[...], preferred_element_type=F32))

    def finish(zz):
        for half in (0, 1):
            h_copy(zz, half).wait_recv()

        @pl.loop(0, 16, unroll=2)
        def _(o):
            v = fbuf[zz, o] + xhr[zz, o].astype(F32)
            rest = v[64:80]
            for m in range(4):
                main = v[16 * m:16 * m + 16]
                even = jnp.where(lane16 < 64, main, pltpu.roll(rest, (128 - 16 * m) % 128, 1))
                odd = jnp.where(lane16 < 64, pltpu.roll(main, 64, 1), pltpu.roll(rest, 64 - 16 * m, 1))
                base = (o * 8 + 2 * m) * 16
                ubuf[pl.ds(pl.multiple_of(base, 16), 16), :] = even
                ubuf[pl.ds(pl.multiple_of(base + 16, 16), 16), :] = odd

        @pl.loop(0, 16, unroll=4)
        def _(r):
            u = ubuf[pl.ds(r, 128, stride=16), :]
            u = u - jnp.mean(u, axis=0, keepdims=True)
            spread = jnp.mean(u * u, axis=0, keepdims=True)
            u = (u * lax.rsqrt(spread + EPS) * gain_col).T[0:80].astype(BF)
            v = jnp.dot(u, o_w[...], preferred_element_type=F32)
            out[zz * 16 + r] = (gates[zz * 16 + r] * v).astype(BF)

    gain_col = jnp.broadcast_to(out_gain[...], (128, 128)).T

    group([0], 1)
    group([0], 0)
    serve(1, 1)
    relay([0], 1)
    relay([0], 0)
    group([1, 7], 1)
    serve(1, 0)
    group([1, 7], 0)
    serve(1, 2)
    relay([1, 7], 1)
    serve_x(2)
    serve_x(6)
    relay([1, 7], 0)
    collect([0], 1)
    collect([0], 0)
    group([2, 6], 1)
    serve(2, 1)
    group([2, 6], 0)
    serve(2, 0)
    make_gates()
    relay([2, 6], 1)
    relay([2, 6], 0)
    collect([1, 7], 1)
    collect([1, 7], 0)
    serve(2, 2)
    serve_x(3)
    serve_x(5)
    group([3, 5], 1)
    serve(3, 1)
    group([3, 5], 0)
    relay([3, 5], 1)
    collect([2, 6], 1)
    serve(3, 0)
    serve(3, 2)
    relay([3, 5], 0)
    serve_x(4)
    group([4], 0)
    group([4], 1)
    collect([2, 6], 0)
    relay([4], 0)
    relay([4], 1)
    collect([3, 5], 1)
    collect([3, 5], 0)

    place = (z + 8 - ((y % 2) * 4 + xh * 2)) % 8
    far = jnp.where((place >= 1) & (place <= 4), 0, 1)
    finish(1 - far)
    collect([4], 0)
    collect([4], 1)
    finish(far)

    for copy in sent:
        copy.wait_send()
    for half in (0, 1):
        for zz in (0, 1):
            h_copy(zz, half).wait_send()
        for cx in (0, 1):
            for o in range(8):
                target, rel, copy = y_copy(cx, at(o), half)

                @pl.when(target != y)
                def _():
                    copy.wait_send()


def step(pair, in_gain, a_w, b_w, g_w, out_gain, o_w):
    vmem = pl.BlockSpec(memory_space=pltpu.VMEM)
    dma = pltpu.SemaphoreType.DMA
    return pl.pallas_call(
        kernel,
        out_shape=jax.ShapeDtypeStruct((32, 80, 128), BF),
        in_specs=[pl.BlockSpec(memory_space=pl.ANY)] + [vmem] * 6,
        out_specs=vmem,
        scratch_shapes=[
            pltpu.VMEM((320, 16, 128), BF),
            pltpu.VMEM((2, KB, 80, 128), BF),
            pltpu.VMEM((4, 8, 80, 128), BF),
            pltpu.VMEM((256, 128), BF),
            pltpu.VMEM((256, 128), BF),
            pltpu.VMEM((3072, 128), F32),
            pltpu.VMEM((3072, 128), F32),
            pltpu.VMEM((2048, 128), F32),
            pltpu.VMEM((32, 32, 80, 128), BF),
            pltpu.VMEM((32, 2, 384, 256), BF),
            pltpu.VMEM((16, 16, 80, 128), BF),
            pltpu.VMEM((4, 4, 16, 80, 128), BF),
            pltpu.VMEM((2, 16, 80, 128), BF),
            pltpu.VMEM((2, 16, 80, 128), BF),
            pltpu.VMEM((2, 16, 80, 128), F32),
            pltpu.VMEM((2048, 128), F32),
            pltpu.VMEM((32, 80, 128), F32),
            dma, dma((2,)), dma((4,)),
            dma((2, 4, 3)), dma((2, 4, 3)),
            dma((10,)), dma((10,)),
            dma((2, 8, 4)), dma((2, 8, 4)),
            dma((16, 2)), dma((4, 4, 2)),
            dma((2, 2)), dma((2, 2)),
        ],
        compiler_params=pltpu.CompilerParams(
            collective_id=0, has_side_effects=True, vmem_limit_bytes=63 * 2 ** 20),
        name="triangle",
    )(pair, in_gain.reshape(1, 128), a_w, b_w, g_w, out_gain.reshape(1, 128), o_w)


def solution(mesh):
    in_specs = (P("row", "col", None), P(), P(), P(), P(), P(), P())
    return jax.shard_map(step, mesh=mesh, in_specs=in_specs, out_specs=P("row", "col", None), check_vma=False)
```
